32 devices in a mesh: sec: 4 (over y, core), dp: 4 (over z), mp: 2 (over x).
Axes of the slice: x: 2, y: 2, z: 4, core: 2. Of those that a mesh axis runs over, the one named last changes fastest.
Arguments:
- policy_query: bfloat16 [16, 128, 4096], P(('sec', 'dp'), None, 'mp'), may hold values from -6 to 6
- policy_memory: bfloat16 [2, 16, 128, 1024], P(None, ('sec', 'dp'), None, 'mp'), may hold values from -6 to 6
- chosen_output_rows: bfloat16 [16, 128, 4096], P(('sec', 'dp'), None, 'mp'), may hold values from -0.09375 to 0.09375
- adapter_rows: bfloat16 [16, 128, 8192], P(('sec', 'dp'), None, 'mp'), may hold values from -6 to 6
- adapter_down: bfloat16 [4096, 64], P('mp'), may hold values from -0.09375 to 0.09375
- adapter_up: bfloat16 [64, 8192], P(None, 'mp'), may hold values from -0.0078125 to 0.0078125
- scorer_query: bfloat16 [4, 4, 4, 128, 4096], P('sec', None, 'dp', None, 'mp'), may hold values from -6 to 6
- scorer_key_values: bfloat16 [4, 2, 4, 4, 128, 1024], P('sec', None, None, 'dp', None, 'mp'), may hold values from -6 to 6
- score_heads: float32 [2, 4096], P(None, 'mp'), may hold values from -0.1875 to 0.1875
- document_ids: int32 [4, 4, 128], P(None, 'dp'), may hold values from 0 to 3, never falling along the last dimension, each value on 1 to 64 neighbouring positions
- prompt_lengths: int32 [4, 4, 4], P(None, 'dp'), may hold values from 1 to 31
Outputs:
- advantages: float32 [16, 128], P(('sec', 'dp'))
- query_grad: bfloat16 [16, 128, 4096], P(('sec', 'dp'), None, 'mp')
- memory_grad: bfloat16 [2, 16, 128, 1024], P(None, ('sec', 'dp'), None, 'mp')
- down_grad: float32 [4096, 64], P('mp')
- up_grad: float32 [64, 8192], P(None, 'mp')
The draws below stay inside these ranges and needn't reach their ends.
Inputs may be any that keep to these rules, and one draw needn't show every extreme that they name: `document_ids`: within each row the document numbers never fall; every document has 1 to 64 positions and one has exactly 64.
All inputs are finite; a program needn't handle non-finite values.
Results may differ from the reference program's by a relative error of at most 0.0081.
Values may be sent and summed in bfloat16 or wider, within the bound.
A program may use at most 64 MiB of HBM per device.

```python
import math
import jax
import jax.numpy as jnp
import numpy as np
from jax import lax

D = 8192
HEAD_DIM = 128
RANK = 64
DOCS = 4
ROW_TOKENS = 128
SECTIONS = 4
DP_ROWS = 4
PACKED_ROWS = 16
HQ = 4096
KEY_FEATURES = 1024


def draw_policy_query(key, part):
    shape = (PACKED_ROWS, ROW_TOKENS, HQ)
    return jnp.clip(jax.random.normal(jax.random.fold_in(key, 101), shape, jnp.float32), -6.0, 6.0).astype(jnp.bfloat16)


def draw_policy_memory(key, part):
    shape = (2, PACKED_ROWS, ROW_TOKENS, KEY_FEATURES)
    return jnp.clip(jax.random.normal(jax.random.fold_in(key, 202), shape, jnp.float32), -6.0, 6.0).astype(jnp.bfloat16)


def draw_scorer_query(key, part):
    shape = (SECTIONS, SECTIONS, DP_ROWS, ROW_TOKENS, HQ)
    return jnp.clip(jax.random.normal(jax.random.fold_in(key, 303), shape, jnp.float32), -6.0, 6.0).astype(jnp.bfloat16)


def draw_scorer_key_values(key, part):
    shape = (SECTIONS, 2, SECTIONS, DP_ROWS, ROW_TOKENS, KEY_FEATURES)
    return jnp.clip(jax.random.normal(jax.random.fold_in(key, 404), shape, jnp.float32), -6.0, 6.0).astype(jnp.bfloat16)


def touch_ends(array, own_key, low, high):
    place = [jax.random.randint(jax.random.fold_in(own_key, axis), (), 0, length) for axis, length in enumerate(array.shape)]
    main_axis = array.shape.index(max(array.shape))
    neighbour = place[:main_axis] + [(place[main_axis] + 1) % array.shape[main_axis]] + place[main_axis + 1:]
    return array.at[tuple(place)].set(low).at[tuple(neighbour)].set(high)


def block_levels(rng, dims, pieces, low, top_value):
    factor_of, own = 1.0, jax.random.fold_in(rng, 6)
    for dim, parts in pieces:
        steps = jnp.exp(jax.random.uniform(jax.random.fold_in(own, dim), (parts,), jnp.float32, low / len(pieces), top_value / len(pieces)))
        factor_of = factor_of * jnp.repeat(steps, dims[dim] // parts).reshape([-1 if axis == dim else 1 for axis in range(len(dims))])
    return factor_of


def profile(count, total, bound, lean):
    loads = [(1 << 20) // math.isqrt(rank ** lean) + 1 for rank in range(2, count + 1)]
    surplus, given = total - bound - (count - 1), [1] * (count - 1)
    while surplus > 0:
        candidates = [i for i in range(count - 1) if given[i] < bound]
        pool, remaining = sum([loads[i] for i in candidates]), surplus
        for i in candidates:
            extra = min(bound - given[i], max(1, remaining * loads[i] // pool), surplus)
            given[i] = given[i] + extra
            surplus = surplus - extra
    return np.array([bound] + given)


def uneven(stream_key, count, total, reach, slope):
    if count == 2:
        one = jax.random.randint(stream_key, (), max(1, total - reach), min(reach, total - 1) + 1)
        return jnp.stack([one, total - one])
    lengths = jnp.asarray(profile(count, total, reach, slope), jnp.int32)
    couples = (count - 1) // 2
    giver, receiver = lengths[1:1 + 2 * couples:2], lengths[2:2 + 2 * couples:2]
    room = jnp.minimum(giver - 1, reach - receiver)
    moved = jax.random.randint(jax.random.fold_in(stream_key, 1), (couples,), 0, 1 << 20) % (room + 1)
    lengths = lengths.at[1:1 + 2 * couples:2].set(giver - moved).at[2:2 + 2 * couples:2].set(receiver + moved)
    return lengths[jax.random.permutation(jax.random.fold_in(stream_key, 2), count)]


def scatter_about(key, extent, scale, reach, split=(), held_as=jnp.bfloat16):
    gain = block_levels(key, extent, split, -0.22, 0.18) if split else 1.0
    values = jax.random.normal(key, extent, jnp.float32) * scale * gain
    return jnp.minimum(jnp.maximum(values, -reach), reach).astype(held_as)


def setup_inputs(seed: int = 0) -> dict:
    streams_of = jax.random.split(jax.random.key(seed), 12)
    policy_query = draw_policy_query(jax.random.fold_in(streams_of[11], 71), 0)
    policy_memory = draw_policy_memory(jax.random.fold_in(streams_of[11], 71), 0)
    chosen_output_rows = scatter_about(streams_of[2], (PACKED_ROWS, ROW_TOKENS, HQ), HQ ** -0.5, 0.09375, ((0, 16), (2, 2)))
    adapter_rows = scatter_about(streams_of[3], (PACKED_ROWS, ROW_TOKENS, D), 1.0, 6.0, ((0, 16), (2, 2)))
    adapter_down = scatter_about(streams_of[4], (HQ, RANK), HQ ** -0.5, 0.09375, ((0, 2),))
    adapter_up = scatter_about(streams_of[5], (RANK, D), (D * RANK) ** -0.5, 0.0078125, ((1, 2),))
    scorer_query = draw_scorer_query(jax.random.fold_in(streams_of[11], 71), 0)
    scorer_key_values = draw_scorer_key_values(jax.random.fold_in(streams_of[11], 71), 0)
    score_heads = scatter_about(streams_of[8], (2, HQ), (HQ // 4) ** -0.5, 0.1875, ((1, 2),), jnp.float32)
    document_ids = jax.vmap(lambda own: jnp.searchsorted(jnp.cumsum(uneven(own, DOCS, ROW_TOKENS, ROW_TOKENS // 2, 0)), jnp.arange(ROW_TOKENS), side="right"))(jax.random.split(streams_of[9], SECTIONS * DP_ROWS)).reshape((SECTIONS, DP_ROWS, ROW_TOKENS)).astype(jnp.int32)
    prompt_lengths = touch_ends(jax.random.randint(streams_of[10], (SECTIONS, DP_ROWS, DOCS), 1, ROW_TOKENS // 4), jax.random.fold_in(streams_of[10], 1), 1, (ROW_TOKENS // 4) - 1).astype(jnp.int32)
    return {"policy_query": policy_query, "policy_memory": policy_memory, "chosen_output_rows": chosen_output_rows, "adapter_rows": adapter_rows, "adapter_down": adapter_down, "adapter_up": adapter_up, "scorer_query": scorer_query, "scorer_key_values": scorer_key_values, "score_heads": score_heads, "document_ids": document_ids, "prompt_lengths": prompt_lengths}


kl_weight = 0.1
trace_decay = 0.95
epsilon = 1e-05
masked_score = -1e+30

def span_masks(document_index, prompt):
    length = document_index.shape[-1]
    labels = jnp.arange(prompt.shape[-1], dtype=jnp.int32)
    member = (document_index[:, None] == labels[None, :]).astype(jnp.float32)
    counts = lax.optimization_barrier(jnp.sum(member, axis=0))
    firsts = jnp.cumsum(counts) - counts
    position = jnp.arange(length).astype(jnp.float32)
    start_pos = lax.optimization_barrier(jnp.sum(member * firsts[None, :], axis=1))
    prompt_pos = lax.optimization_barrier(jnp.sum(member * prompt.astype(jnp.float32)[None, :], axis=1))
    ending = lax.optimization_barrier(jnp.sum(member * (firsts + counts - 1.0)[None, :], axis=1))
    respond = (position - start_pos >= prompt_pos).astype(jnp.float32)
    closing = (position == ending).astype(jnp.float32)
    return (respond, closing)

def trace_matrix(document_index):
    length = document_index.shape[-1]
    position = jnp.arange(length, dtype=jnp.int32)
    later = position[None, :] - position[:, None]
    linked = (document_index[:, None] == document_index[None, :]) & (later >= 0)
    powers = jnp.power(jnp.float32(trace_decay), jnp.maximum(later, 0).astype(jnp.float32))
    return jnp.where(linked, powers, jnp.float32(0.0))

def attend_section(query, keys, values, document_index):
    length = query.shape[0]
    kv_heads = keys.shape[1] // HEAD_DIM
    groups = query.shape[1] // keys.shape[1]
    query_h = query.reshape(length, kv_heads, groups, HEAD_DIM).astype(jnp.float32)
    keys_h = keys.reshape(length, kv_heads, HEAD_DIM).astype(jnp.float32)
    values_h = values.reshape(length, kv_heads, HEAD_DIM).astype(jnp.float32)
    scores = jnp.einsum('qcgd,kcd->cgqk', query_h, keys_h) * HEAD_DIM ** (-0.5)
    position = jnp.arange(length, dtype=jnp.int32)
    allowed = (document_index[:, None] == document_index[None, :]) & (position[:, None] >= position[None, :])
    scores = jnp.where(allowed, scores, masked_score)
    top = lax.optimization_barrier(jnp.max(scores, axis=-1, keepdims=True))
    raised = jnp.exp(scores - top)
    probs = raised / lax.optimization_barrier(jnp.sum(raised, axis=-1, keepdims=True))
    probs_b = probs.astype(jnp.bfloat16)
    attended = jnp.einsum('cgqk,kcd->qcgd', probs_b.astype(jnp.float32), values_h).reshape(length, -1)
    return (attended, probs, probs_b)

def attend_back(query, keys, values, probs, probs_b, grad_b):
    length = query.shape[0]
    kv_heads = keys.shape[1] // HEAD_DIM
    groups = query.shape[1] // keys.shape[1]
    query_h = query.reshape(length, kv_heads, groups, HEAD_DIM).astype(jnp.float32)
    keys_h = keys.reshape(length, kv_heads, HEAD_DIM).astype(jnp.float32)
    values_h = values.reshape(length, kv_heads, HEAD_DIM).astype(jnp.float32)
    grad_h = grad_b.reshape(length, kv_heads, groups, HEAD_DIM).astype(jnp.float32)
    dprobs = jnp.einsum('qcgd,kcd->cgqk', grad_h, values_h)
    inner = lax.optimization_barrier(jnp.sum(probs * dprobs, axis=-1, keepdims=True))
    dscores = (probs * (dprobs - inner)).astype(jnp.bfloat16).astype(jnp.float32)
    scale = HEAD_DIM ** (-0.5)
    query_grad = (jnp.einsum('cgqk,kcd->qcgd', dscores, keys_h) * scale).astype(jnp.bfloat16).reshape(length, -1)
    keys_grad = (jnp.einsum('cgqk,qcgd->kcd', dscores, query_h) * scale).astype(jnp.bfloat16).reshape(length, -1)
    values_grad = jnp.einsum('cgqk,qcgd->kcd', probs_b.astype(jnp.float32), grad_h).astype(jnp.bfloat16).reshape(length, -1)
    return (query_grad, keys_grad, values_grad)

def reference(policy_query, policy_memory, chosen_output_rows, adapter_rows, adapter_down, adapter_up, scorer_query, scorer_key_values, score_heads, document_ids, prompt_lengths):
    highest = lax.Precision.HIGHEST
    document_list = document_ids.reshape(PACKED_ROWS, ROW_TOKENS)
    prompts = prompt_lengths.reshape(PACKED_ROWS, DOCS)
    down_float = adapter_down.astype(jnp.float32)

    def forward_row(item_list):
        query, keys, values, document_index, chosen_token, adapter = item_list
        attended, probs, probs_b = attend_section(query, keys, values, document_index)
        base = lax.optimization_barrier(jnp.sum(attended * chosen_token.astype(jnp.float32), axis=1))
        lowrank_in = jnp.dot(attended, down_float, precision=highest)
        lowrank_out = jnp.dot(adapter, adapter_up.T, preferred_element_type=jnp.float32)
        return (base, lowrank_in, lowrank_out)
    base, lowrank_in, lowrank_out = lax.map(forward_row, (policy_query, policy_memory[0], policy_memory[1], document_list, chosen_output_rows, adapter_rows))
    policy_new = base + lax.optimization_barrier(jnp.sum(lowrank_in * lowrank_out, axis=-1))
    per_section_scores = []
    for section_index in range(4):
        scorer_query_rows = scorer_query[section_index].reshape(PACKED_ROWS, ROW_TOKENS, HQ)
        scorer_keys = scorer_key_values[section_index, 0].reshape(PACKED_ROWS, ROW_TOKENS, KEY_FEATURES)
        scorer_values = scorer_key_values[section_index, 1].reshape(PACKED_ROWS, ROW_TOKENS, KEY_FEATURES)
        if section_index < 2:

            def score_row_values(item_list):
                query, keys, values, document_index, chosen_token = item_list
                attended, probs, probs_b = attend_section(query, keys, values, document_index)
                return lax.optimization_barrier(jnp.sum(attended * chosen_token.astype(jnp.float32), axis=1))
            per_section_scores.append(lax.map(score_row_values, (scorer_query_rows, scorer_keys, scorer_values, document_list, chosen_output_rows)))
        else:
            head = score_heads[section_index - 2]

            def head_row_index(item_list):
                query, keys, values, document_index = item_list
                attended, probs, probs_b = attend_section(query, keys, values, document_index)
                return jnp.dot(attended, head, precision=highest)
            per_section_scores.append(lax.map(head_row_index, (scorer_query_rows, scorer_keys, scorer_values, document_list)))
    policy_old, policy_ref, reward, value = per_section_scores
    respond, closing = jax.vmap(span_masks)(document_list, prompts)
    next_value = jnp.concatenate([value[:, 1:], jnp.zeros((PACKED_ROWS, 1), jnp.float32)], axis=1) * (1.0 - closing)
    delta = -kl_weight * (policy_old - policy_ref) + closing * reward + next_value - value
    matrices = jax.vmap(trace_matrix)(document_list)
    advantage = jnp.einsum('rtu,ru->rt', matrices, delta, precision=highest)
    count = jnp.sum(respond)
    total = jnp.sum(respond * advantage)
    square_total = jnp.sum(respond * advantage * advantage)
    mean = total / count
    spread = square_total / count - mean * mean
    whitened = respond * (advantage - mean) * lax.rsqrt(spread + epsilon)
    ratio = jnp.exp(policy_new - policy_old)
    grad_score = -respond * ratio * whitened / count

    def backward_row(carry, item_list):
        query, keys, values, document_index, chosen_token, adapter, gscore, low_in, low_out = item_list
        attended, probs, probs_b = attend_section(query, keys, values, document_index)
        scaled_out = gscore[:, None] * low_out
        grad_attended = (gscore[:, None] * chosen_token.astype(jnp.float32) + jnp.dot(scaled_out, down_float.T, precision=highest)).astype(jnp.bfloat16)
        down_term = jnp.dot(attended.T, scaled_out, precision=highest)
        scaled_in = (gscore[:, None] * low_in).astype(jnp.bfloat16)
        up_term = jnp.dot(scaled_in.T, adapter, preferred_element_type=jnp.float32)
        grads = attend_back(query, keys, values, probs, probs_b, grad_attended)
        return ((carry[0] + down_term, carry[1] + up_term), grads)
    start = (jnp.zeros((HQ, RANK), jnp.float32), jnp.zeros((RANK, D), jnp.float32))
    sums, grads = lax.scan(backward_row, start, (policy_query, policy_memory[0], policy_memory[1], document_list, chosen_output_rows, adapter_rows, grad_score, lowrank_in, lowrank_out))
    query_grad, keys_grad, values_grad = grads
    return (whitened, query_grad, jnp.stack([keys_grad, values_grad]), sums[0], sums[1])
```

```python
import functools
import math

import jax
import jax.numpy as jnp
from jax import lax
from jax.experimental import pallas as pl
from jax.experimental.pallas import tpu as pltpu
from jax.sharding import PartitionSpec as P

HEAD_DIM = 128
kl_weight = 0.1
trace_decay = 0.95
epsilon = 1e-05
masked_score = -1e30
F32, BF16 = jnp.float32, jnp.bfloat16
MESH = pl.DeviceIdType.MESH


def nn(a, b):
    return jnp.dot(a, b, preferred_element_type=F32)


def nt(a, b):
    return lax.dot_general(a, b, (((1,), (1,)), ((), ())), preferred_element_type=F32)


def tn(a, b):
    return lax.dot_general(a, b, (((0,), (0,)), ((), ())), preferred_element_type=F32)


def split(a):
    high = a.astype(BF16)
    return high, (a - high.astype(F32)).astype(BF16)


def kernel(S, N, M, L,
           q_ref, kv_ref, chosen_ref, rows_ref, down_ref, up_ref, sq_ref, skv_ref, heads_ref, docs_ref, prompts_ref,
           adv_ref, qg_ref, mg_ref, dg_ref, ug_ref,
           att, patt, probs, chosen_rx, score_tx, score_rx, pack_tx, pack_rx, mom_rx,
           both, tx1, rx1, tx2, rx2, txz, rxz, fin, grad,
           c_send, c_recv, s_send, s_recv, p_send, p_recv, m_send, m_recv, h_send, h_recv, z_send, z_recv, g_send,
           g_recv, a_send, a_recv):
    T = q_ref.shape[0]
    HQ = q_ref.shape[1]
    KV = kv_ref.shape[2]
    heads = KV // HEAD_DIM
    groups = HQ // KV
    RANK = down_ref.shape[1]
    DOCS = prompts_ref.shape[2]
    sec, dp, mp = lax.axis_index("sec"), lax.axis_index("dp"), lax.axis_index("mp")
    scale = HEAD_DIM ** (-0.5)

    def add(x, d, n):
        return lax.rem(x + d, n) if d else x

    offsets = [(s, d, 0) for s in range(S) for d in range(N) if s or d]
    offsets += [(s, 0, m) for s in range(S) for m in range(1, M)]
    barrier = pltpu.get_barrier_semaphore()
    for s, d, m in offsets:
        pl.semaphore_signal(barrier, inc=1, device_id=(add(sec, s, S), add(dp, d, N), add(mp, m, M)),
                            device_id_type=MESH)
    pl.semaphore_wait(barrier, len(offsets))

    half = S // 2
    pair = 1 - lax.rem(sec, 2)

    def chosen_copy(src, slot, k, target):
        return pltpu.make_async_remote_copy(src, chosen_rx.at[slot], c_send.at[k], c_recv.at[k],
                                            device_id=(target, dp, mp), device_id_type=MESH)

    @pl.when(sec >= half)
    def _():
        chosen_copy(chosen_ref, sec, 0, lax.rem(sec, half)).start()

    @pl.when(sec < half)
    def _():
        chosen_copy(chosen_ref, sec, 1, pair).start()
        chosen_rx[sec] = chosen_ref[...]

    q_pos = lax.broadcasted_iota(jnp.int32, (T, T), 0)
    k_pos = lax.broadcasted_iota(jnp.int32, (T, T), 1)

    def docs_of(j):
        row = jnp.broadcast_to(docs_ref[j].astype(F32), (T, T))
        return row, row.T

    def attend(q, k, v, allowed):
        scores = jnp.where(allowed, nt(q, k) * scale, masked_score)
        raised = jnp.exp(scores - jnp.max(scores, axis=-1, keepdims=True))
        p = raised * (1.0 / jnp.sum(raised, axis=-1, keepdims=True))
        return p, nn(p.astype(BF16), v)

    def stack(ref, c):
        return jnp.concatenate(
            [ref[:, (c * groups + g) * HEAD_DIM:(c * groups + g + 1) * HEAD_DIM] for g in range(groups)], axis=0)

    def score_row(j, carry):
        row, col = docs_of(j)
        allowed = jnp.concatenate([(row == col) & (q_pos >= k_pos)] * groups, axis=0)
        for c in range(heads):
            cs = slice(c * HEAD_DIM, (c + 1) * HEAD_DIM)
            _, out = attend(stack(sq_ref.at[j], c), skv_ref[0, j, :, cs], skv_ref[1, j, :, cs], allowed)
            att[j, c] = out
        return carry

    lax.fori_loop(0, S, score_row, 0)

    @pl.when(sec < half)
    def _():
        chosen_copy(chosen_ref, sec, 0, pair).wait_recv()
        chosen_copy(chosen_rx.at[sec + half], sec + half, 2, pair).start()

    row, col = docs_of(sec)
    allowed = jnp.concatenate([(row == col) & (q_pos >= k_pos)] * groups, axis=0)
    base_acc = jnp.zeros((T, HEAD_DIM), F32)
    low_in = jnp.zeros((T, RANK), F32)
    for c in range(heads):
        cs = slice(c * HEAD_DIM, (c + 1) * HEAD_DIM)
        p, out = attend(stack(q_ref, c), kv_ref[0, :, cs], kv_ref[1, :, cs], allowed)
        probs[c] = p
        for g in range(groups):
            hs = slice((c * groups + g) * HEAD_DIM, (c * groups + g + 1) * HEAD_DIM)
            part = out[g * T:(g + 1) * T]
            patt[:, hs] = part
            base_acc += part * chosen_ref[:, hs].astype(F32)
    high, low = split(patt[...])
    low_in = nn(high, down_ref[...]) + nn(low, down_ref[...])
    low_out = nt(rows_ref[...], up_ref[...])
    pack_tx[...] = jnp.concatenate([low_in, low_out], axis=1)

    def pack_copy(m):
        return pltpu.make_async_remote_copy(pack_tx, pack_rx.at[m], p_send.at[m], p_recv.at[m],
                                            device_id=(sec, dp, add(mp, m, M)), device_id_type=MESH)

    for m in range(1, M):
        pack_copy(m).start()

    columns = jnp.where(k_pos == S, jnp.sum(base_acc, axis=1, keepdims=True), 0.0)
    grad[...] = columns

    @pl.when(sec < half)
    def _():
        chosen_copy(chosen_ref, sec, 1, pair).wait_recv()
        chosen_copy(chosen_ref, sec, 2, pair).wait_recv()
        for j in range(S):
            acc = jnp.zeros((T, HEAD_DIM), F32)
            for c in range(heads):
                for g in range(groups):
                    h = c * groups + g
                    acc += att[j, c, g * T:(g + 1) * T, :] * chosen_rx[
                        j, :, h * HEAD_DIM:(h + 1) * HEAD_DIM].astype(F32)
            grad[...] += jnp.where(k_pos == j, jnp.sum(acc, axis=1, keepdims=True), 0.0)

    @pl.when(sec >= half)
    def _():
        for j in range(S):
            acc = jnp.zeros((T, HEAD_DIM), F32)
            for c in range(heads):
                for g in range(groups):
                    h = c * groups + g
                    both_heads = heads_ref[:, h * HEAD_DIM:(h + 1) * HEAD_DIM]
                    acc += att[j, c, g * T:(g + 1) * T, :] * jnp.where(
                        sec == half, both_heads[0:1], both_heads[1:2])
            grad[...] += jnp.where(k_pos == j, jnp.sum(acc, axis=1, keepdims=True), 0.0)

    turned = grad[...].T
    sub = lax.broadcasted_iota(jnp.int32, (8, T), 0)
    for j in range(S):
        score_tx[j] = jnp.where(sub == 0, turned[j:j + 1, :], turned[S:S + 1, :])

    def score_copy(s, m):
        target = add(sec, s, S)
        return pltpu.make_async_remote_copy(score_tx.at[target], score_rx.at[s * M + m], s_send.at[s * M + m],
                                            s_recv.at[s * M + m],
                                            device_id=(target, dp, add(mp, m, M)), device_id_type=MESH)

    score_rx[0] = score_tx[sec]
    pairs = [(s, m) for s in range(S) for m in range(M) if s or m]
    for s, m in pairs:
        score_copy(s, m).start()

    lane = lax.broadcasted_iota(jnp.int32, (1, T), 1)
    doc = docs_ref[sec]
    start_pos = jnp.sum((col < row).astype(F32), axis=0, keepdims=True)
    ending = jnp.sum((col <= row).astype(F32), axis=0, keepdims=True) - 1.0
    prompt_row = prompts_ref[sec]
    prompt_pos = jnp.zeros((1, T), F32)
    for d in range(DOCS):
        prompt_pos += jnp.where(doc == d, prompt_row[:, d:d + 1].astype(F32), 0.0)
    position = lane.astype(F32)
    respond = (position - start_pos >= prompt_pos).astype(F32)
    closing = (position == ending).astype(F32)
    later = q_pos - k_pos
    trace = jnp.where((row == col) & (later >= 0),
                      jnp.exp(jnp.maximum(later, 0).astype(F32) * math.log(trace_decay)), 0.0)

    for m in range(1, M):
        pack_copy(m).wait()
    packed = pack_tx[...]
    for m in range(1, M):
        packed = packed + pack_rx[m]
    low_in, low_out = packed[:, :RANK], packed[:, RANK:]
    low_sum = jnp.broadcast_to(jnp.sum(low_in * low_out, axis=1, keepdims=True), (T, T)).T[0:1, :]

    for s, m in pairs:
        score_copy(s, m).wait()

    def section(k):
        slot = lax.rem(sec - k + S, S) * M
        total = score_rx[slot]
        for m in range(1, M):
            total = total + score_rx[slot + m]
        return total[0:1, :]

    base = score_rx[0]
    for m in range(1, M):
        base = base + score_rx[m]
    policy_new = base[1:2, :] + low_sum
    old, ref, reward, value = section(0), section(1), section(2), section(3)
    value8 = jnp.broadcast_to(value, (8, T))
    next_value = jnp.where(lane == T - 1, 0.0, pltpu.roll(value8, T - 1, 1)[0:1, :]) * (1.0 - closing)
    delta = -kl_weight * (old - ref) + closing * reward + next_value - value
    advantage = jnp.sum(trace * jnp.broadcast_to(delta, (T, T)).T, axis=0, keepdims=True)
    count = jnp.sum(respond, axis=1, keepdims=True)
    total = jnp.sum(respond * advantage, axis=1, keepdims=True)
    square = jnp.sum(respond * advantage * advantage, axis=1, keepdims=True)
    mom_rx[0] = jnp.where(sub == 0, count, jnp.where(sub == 1, total, square))

    def mom_copy(s, d):
        k = s * N + d
        return pltpu.make_async_remote_copy(mom_rx.at[0], mom_rx.at[k], m_send.at[k], m_recv.at[k],
                                            device_id=(add(sec, s, S), add(dp, d, N), mp), device_id_type=MESH)

    peers = [(s, d) for s in range(S) for d in range(N) if s or d]
    for s, d in peers:
        mom_copy(s, d).start()
    for s, d in peers:
        mom_copy(s, d).wait()
    moments = jnp.sum(mom_rx[...], axis=0)
    count, total, square = moments[0:1], moments[1:2], moments[2:3]
    mean = total / count
    spread = square / count - mean * mean
    whitened = respond * (advantage - mean) * lax.rsqrt(spread + epsilon)
    adv_ref[...] = whitened
    grad_score = -respond * jnp.exp(policy_new - old) * whitened / count
    gs = jnp.broadcast_to(grad_score, (T, T)).T

    scaled_out = gs[:, :RANK] * low_out
    scaled_in = gs[:, :RANK] * low_in
    turned = jnp.concatenate([scaled_out, scaled_in], axis=1).T
    out_high, out_low = split(turned[:RANK])
    in_t = turned[RANK:].astype(BF16)
    D = rows_ref.shape[1]
    for p in range(S * N):
        lo, hi = p * L, (p + 1) * L
        a, b = min(lo, HQ), min(hi, HQ)
        if b > a:
            high, low = split(patt[:, a:b])
            both[p, :, a - lo:b - lo] = nn(out_high, high) + nn(out_low, high) + nn(out_high, low)
        a, b = max(lo, HQ), min(hi, HQ + D)
        if b > a:
            both[p, :, a - lo:b - lo] = nn(in_t, rows_ref[:, a - HQ:b - HQ])
        a = max(lo, HQ + D)
        if hi > a:
            both[p, :, a - lo:] = jnp.zeros((RANK, hi - a), F32)

    b0, b1 = lax.rem(sec, 2), sec // 2
    near, far = sec + 1 - 2 * b0, lax.rem(sec + half, S)
    Q, H = N, 2 * N

    def block_copy(src, dst, k, target):
        return pltpu.make_async_remote_copy(src, dst, h_send.at[k], h_recv.at[k],
                                            device_id=(target, dp, mp), device_id_type=MESH)

    tx1[...] = both[pl.ds((1 - b0) * H, H)].astype(BF16)
    copy1 = block_copy(tx1, rx1, 0, near)
    copy1.start()

    so_high, so_low = split(scaled_out)

    def back(c):
        cs = slice(c * HEAD_DIM, (c + 1) * HEAD_DIM)
        down_c = down_ref[c * groups * HEAD_DIM:(c + 1) * groups * HEAD_DIM, :]
        through = nt(so_high, down_c) + nt(so_low, down_c)
        g = jnp.concatenate(
            [gs * chosen_ref[:, (c * groups + i) * HEAD_DIM:(c * groups + i + 1) * HEAD_DIM].astype(F32)
             + through[:, i * HEAD_DIM:(i + 1) * HEAD_DIM] for i in range(groups)], axis=0).astype(BF16)
        p = probs[c]
        k, v = kv_ref[0, :, cs], kv_ref[1, :, cs]
        dprobs = nt(g, v)
        inner = jnp.sum(p * dprobs, axis=-1, keepdims=True)
        ds = (p * (dprobs - inner)).astype(BF16)
        qg = (nn(ds, k) * scale).astype(BF16)
        for i in range(groups):
            qg_ref[:, (c * groups + i) * HEAD_DIM:(c * groups + i + 1) * HEAD_DIM] = qg[i * T:(i + 1) * T]
        mg_ref[0, :, cs] = (tn(ds, stack(q_ref, c)) * scale).astype(BF16)
        mg_ref[1, :, cs] = tn(p.astype(BF16), g).astype(BF16)

    todo = list(range(heads))

    def some(n):
        for _ in range(min(n, len(todo))):
            back(todo.pop(0))

    some(1)
    copy1.wait()
    mine = b0 * H
    tx2[...] = (both[pl.ds(mine + (1 - b1) * Q, Q)] + rx1[pl.ds((1 - b1) * Q, Q)].astype(F32)).astype(BF16)
    copy2 = block_copy(tx2, rx2, 1, far)
    copy2.start()
    mine = mine + b1 * Q
    both[pl.ds(mine, Q)] += rx1[pl.ds(b1 * Q, Q)].astype(F32)
    some(2)
    copy2.wait()
    both[pl.ds(mine, Q)] += rx2[...].astype(F32)
    txz[...] = both[pl.ds(mine, Q)].astype(BF16)

    def z_copy(d):
        target = add(dp, d, N)
        return pltpu.make_async_remote_copy(txz.at[target], rxz.at[d], z_send.at[d], z_recv.at[d],
                                            device_id=(sec, target, mp), device_id_type=MESH)

    for d in range(1, N):
        z_copy(d).start()
    some(heads)
    for d in range(1, N):
        z_copy(d).wait()
    own = both[mine + dp]
    for d in range(1, N):
        own = own + rxz[d].astype(F32)
    fin[mine + dp] = own.astype(BF16)

    def g_copy(d):
        return pltpu.make_async_remote_copy(fin.at[mine + dp], fin.at[mine + dp], g_send.at[d], g_recv.at[d],
                                            device_id=(sec, add(dp, d, N), mp), device_id_type=MESH)

    for d in range(1, N):
        g_copy(d).start()
    for d in range(1, N):
        g_copy(d).wait()

    def a_copy(k, start, size, target):
        ref = fin.at[pl.ds(start, size)]
        return pltpu.make_async_remote_copy(ref, ref, a_send.at[k], a_recv.at[k],
                                            device_id=(target, dp, mp), device_id_type=MESH)

    copy3 = a_copy(0, mine, Q, far)
    copy3.start()
    copy3.wait()
    copy4 = a_copy(1, b0 * H, H, near)
    copy4.start()
    copy4.wait()
    for p in range(S * N):
        lo, hi = p * L, (p + 1) * L
        a, b = min(lo, HQ), min(hi, HQ)
        if b > a:
            dg_ref[:, a:b] = fin[p, :, a - lo:b - lo].astype(F32)
        a, b = max(lo, HQ), min(hi, HQ + D)
        if b > a:
            ug_ref[:, a - HQ:b - HQ] = fin[p, :, a - lo:b - lo].astype(F32)

    @pl.when(sec >= half)
    def _():
        chosen_copy(chosen_ref, sec, 0, lax.rem(sec, half)).wait_send()

    @pl.when(sec < half)
    def _():
        chosen_copy(chosen_ref, sec, 1, pair).wait_send()
        chosen_copy(chosen_rx.at[sec + half], sec + half, 2, pair).wait_send()


def on_device(S, N, M, query, memory, chosen, rows, down, up, squery, skv, score_heads, docs, prompts):
    T, HQ = query.shape[1:]
    KV = memory.shape[3]
    D, RANK = rows.shape[2], down.shape[1]
    heads, groups = KV // HEAD_DIM, HQ // KV
    pieces = S * N
    L = -(-(HQ + D) // (pieces * 128)) * 128
    dma = pltpu.SemaphoreType.DMA
    vm = pltpu.VMEM
    outs = pl.pallas_call(
        functools.partial(kernel, S, N, M, L),
        out_shape=(
            jax.ShapeDtypeStruct((1, T), F32),
            jax.ShapeDtypeStruct((T, HQ), BF16),
            jax.ShapeDtypeStruct((2, T, KV), BF16),
            jax.ShapeDtypeStruct((RANK, HQ), F32),
            jax.ShapeDtypeStruct((RANK, D), F32),
        ),
        in_specs=[pl.BlockSpec(memory_space=pltpu.VMEM)] * 11,
        out_specs=[pl.BlockSpec(memory_space=pltpu.VMEM)] * 5,
        scratch_shapes=[
            vm((S, heads, groups * T, HEAD_DIM), F32), vm((T, HQ), F32), vm((heads, groups * T, T), F32),
            vm((S, T, HQ), BF16), vm((S, 8, T), F32), vm((S * M, 8, T), F32), vm((T, 2 * RANK), F32),
            vm((M, T, 2 * RANK), F32), vm((pieces, 8, T), F32),
            vm((pieces, RANK, L), F32), vm((pieces // 2, RANK, L), BF16), vm((pieces // 2, RANK, L), BF16),
            vm((N, RANK, L), BF16), vm((N, RANK, L), BF16), vm((N, RANK, L), BF16), vm((N, RANK, L), BF16),
            vm((pieces, RANK, L), BF16), vm((T, T), F32),
            dma((3,)), dma((3,)), dma((S * M,)), dma((S * M,)), dma((M,)), dma((M,)), dma((pieces,)), dma((pieces,)),
            dma((2,)), dma((2,)), dma((N,)), dma((N,)), dma((N,)), dma((N,)), dma((2,)), dma((2,)),
        ],
        compiler_params=pltpu.CompilerParams(collective_id=0, has_side_effects=True,
                                             vmem_limit_bytes=56 * 1024 * 1024),
    )(query[0], memory[:, 0], chosen[0], rows[0], down, up, squery[0, :, 0], skv[0, :, :, 0], score_heads,
      docs, prompts)
    adv, qg, mg, dg, ug = outs
    return adv, qg[None], mg[:, None], dg.T, ug


def solution(mesh):
    S, N, M = (mesh.shape[a] for a in ("sec", "dp", "mp"))
    return jax.shard_map(
        functools.partial(on_device, S, N, M),
        mesh=mesh,
        in_specs=(
            P(("sec", "dp"), None, "mp"),
            P(None, ("sec", "dp"), None, "mp"),
            P(("sec", "dp"), None, "mp"),
            P(("sec", "dp"), None, "mp"),
            P("mp", None),
            P(None, "mp"),
            P("sec", None, "dp", None, "mp"),
            P("sec", None, None, "dp", None, "mp"),
            P(None, "mp"),
            P(None, "dp", None),
            P(None, "dp", None),
        ),
        out_specs=(
            P(("sec", "dp"), None),
            P(("sec", "dp"), None, "mp"),
            P(None, ("sec", "dp"), None, "mp"),
            P("mp", None),
            P(None, "mp"),
        ),
        check_vma=False,
    )
```

```python
import functools
import math

import jax
import jax.numpy as jnp
from jax import lax
from jax.experimental import pallas as pl
from jax.experimental.pallas import tpu as pltpu
from jax.sharding import PartitionSpec as P

HEAD_DIM = 128
kl_weight = 0.1
trace_decay = 0.95
epsilon = 1e-05
masked_score = -1e30
F32, BF16 = jnp.float32, jnp.bfloat16
MESH = pl.DeviceIdType.MESH


def nn(a, b):
    return jnp.dot(a, b, preferred_element_type=F32)


def nt(a, b):
    return lax.dot_general(a, b, (((1,), (1,)), ((), ())), preferred_element_type=F32)


def tn(a, b):
    return lax.dot_general(a, b, (((0,), (0,)), ((), ())), preferred_element_type=F32)


def split(a):
    high = a.astype(BF16)
    return high, (a - high.astype(F32)).astype(BF16)


def kernel(S, N, M, L,
           q_ref, kv_ref, chosen_ref, rows_ref, down_ref, up_ref, sq_ref, skv_ref, heads_ref, docs_ref, prompts_ref,
           adv_ref, qg_ref, mg_ref, sum_ref,
           att, patt, probs, chosen_rx, score_tx, score_rx, pack_tx, pack_rx, mom_rx,
           both, tx1, rx1, tx2, rx2, txz, rxz, fin, grad,
           c_send, c_recv, s_send, s_recv, p_send, p_recv, m_send, m_recv, h_send, h_recv, f_send, f_recv, z_send, z_recv, g_send,
           g_recv, a_send, a_recv):
    T = q_ref.shape[0]
    HQ = q_ref.shape[1]
    KV = kv_ref.shape[2]
    heads = KV // HEAD_DIM
    groups = HQ // KV
    RANK = down_ref.shape[0]
    DOCS = prompts_ref.shape[2]
    sec, dp, mp = lax.axis_index("sec"), lax.axis_index("dp"), lax.axis_index("mp")
    scale = HEAD_DIM ** (-0.5)

    def add(x, d, n):
        return lax.rem(x + d, n) if d else x

    offsets = [(s, d, 0) for s in range(S) for d in range(N) if s or d]
    offsets += [(s, 0, m) for s in range(S) for m in range(1, M)]
    barrier = pltpu.get_barrier_semaphore()
    for s, d, m in offsets:
        pl.semaphore_signal(barrier, inc=1, device_id=(add(sec, s, S), add(dp, d, N), add(mp, m, M)),
                            device_id_type=MESH)
    pl.semaphore_wait(barrier, len(offsets))

    half = S // 2
    pair = 1 - lax.rem(sec, 2)

    def chosen_copy(src, slot, k, target):
        return pltpu.make_async_remote_copy(src, chosen_rx.at[slot], c_send.at[k], c_recv.at[k],
                                            device_id=(target, dp, mp), device_id_type=MESH)

    @pl.when(sec >= half)
    def _():
        chosen_copy(chosen_ref, sec, 0, lax.rem(sec, half)).start()

    @pl.when(sec < half)
    def _():
        chosen_copy(chosen_ref, sec, 1, pair).start()
        chosen_rx[sec] = chosen_ref[...]

    q_pos = lax.broadcasted_iota(jnp.int32, (T, T), 0)
    k_pos = lax.broadcasted_iota(jnp.int32, (T, T), 1)

    def docs_of(j):
        row = jnp.broadcast_to(docs_ref[j].astype(F32), (T, T))
        return row, row.T

    def attend(q, k, v, allowed):
        scores = jnp.where(allowed, nt(q, k) * scale, masked_score)
        raised = jnp.exp(scores - jnp.max(scores, axis=-1, keepdims=True))
        p = raised * (1.0 / jnp.sum(raised, axis=-1, keepdims=True))
        return p, nn(p.astype(BF16), v)

    def stack(ref, c):
        return jnp.concatenate(
            [ref[:, (c * groups + g) * HEAD_DIM:(c * groups + g + 1) * HEAD_DIM] for g in range(groups)], axis=0)

    def score_row(j, carry):
        row, col = docs_of(j)
        allowed = jnp.concatenate([(row == col) & (q_pos >= k_pos)] * groups, axis=0)
        for c in range(heads):
            cs = slice(c * HEAD_DIM, (c + 1) * HEAD_DIM)
            _, out = attend(stack(sq_ref.at[j], c), skv_ref[0, j, :, cs], skv_ref[1, j, :, cs], allowed)
            att[j, c] = out
        return carry

    lax.fori_loop(0, S, score_row, 0)

    @pl.when(sec < half)
    def _():
        chosen_copy(chosen_ref, sec, 0, pair).wait_recv()
        chosen_copy(chosen_rx.at[sec + half], sec + half, 2, pair).start()

    row, col = docs_of(sec)
    allowed = jnp.concatenate([(row == col) & (q_pos >= k_pos)] * groups, axis=0)
    base_acc = jnp.zeros((T, HEAD_DIM), F32)
    low_in = jnp.zeros((T, RANK), F32)
    for c in range(heads):
        cs = slice(c * HEAD_DIM, (c + 1) * HEAD_DIM)
        p, out = attend(stack(q_ref, c), kv_ref[0, :, cs], kv_ref[1, :, cs], allowed)
        probs[c] = p
        for g in range(groups):
            hs = slice((c * groups + g) * HEAD_DIM, (c * groups + g + 1) * HEAD_DIM)
            part = out[g * T:(g + 1) * T]
            patt[:, hs] = part
            base_acc += part * chosen_ref[:, hs].astype(F32)
    high, low = split(patt[...])
    low_in = nt(high, down_ref[...]) + nt(low, down_ref[...])
    low_out = nt(rows_ref[...], up_ref[...])
    pack_tx[...] = jnp.concatenate([low_in, low_out], axis=1)

    def pack_copy(m):
        return pltpu.make_async_remote_copy(pack_tx, pack_rx.at[m], p_send.at[m], p_recv.at[m],
                                            device_id=(sec, dp, add(mp, m, M)), device_id_type=MESH)

    for m in range(1, M):
        pack_copy(m).start()

    columns = jnp.where(k_pos == S, jnp.sum(base_acc, axis=1, keepdims=True), 0.0)
    grad[...] = columns

    @pl.when(sec < half)
    def _():
        chosen_copy(chosen_ref, sec, 1, pair).wait_recv()
        chosen_copy(chosen_ref, sec, 2, pair).wait_recv()
        for j in range(S):
            acc = jnp.zeros((T, HEAD_DIM), F32)
            for c in range(heads):
                for g in range(groups):
                    h = c * groups + g
                    acc += att[j, c, g * T:(g + 1) * T, :] * chosen_rx[
                        j, :, h * HEAD_DIM:(h + 1) * HEAD_DIM].astype(F32)
            grad[...] += jnp.where(k_pos == j, jnp.sum(acc, axis=1, keepdims=True), 0.0)

    @pl.when(sec >= half)
    def _():
        for j in range(S):
            acc = jnp.zeros((T, HEAD_DIM), F32)
            for c in range(heads):
                for g in range(groups):
                    h = c * groups + g
                    both_heads = heads_ref[:, h * HEAD_DIM:(h + 1) * HEAD_DIM]
                    acc += att[j, c, g * T:(g + 1) * T, :] * jnp.where(
                        sec == half, both_heads[0:1], both_heads[1:2])
            grad[...] += jnp.where(k_pos == j, jnp.sum(acc, axis=1, keepdims=True), 0.0)

    turned = grad[...].T
    sub = lax.broadcasted_iota(jnp.int32, (8, T), 0)
    for j in range(S):
        score_tx[j] = jnp.where(sub == 0, turned[j:j + 1, :], turned[S:S + 1, :])

    def score_copy(s, m):
        target = add(sec, s, S)
        return pltpu.make_async_remote_copy(score_tx.at[target], score_rx.at[s * M + m], s_send.at[s * M + m],
                                            s_recv.at[s * M + m],
                                            device_id=(target, dp, add(mp, m, M)), device_id_type=MESH)

    score_rx[0] = score_tx[sec]
    pairs = [(s, m) for s in range(S) for m in range(M) if s or m]
    for s, m in pairs:
        score_copy(s, m).start()

    lane = lax.broadcasted_iota(jnp.int32, (1, T), 1)
    doc = docs_ref[sec]
    start_pos = jnp.sum((col < row).astype(F32), axis=0, keepdims=True)
    ending = jnp.sum((col <= row).astype(F32), axis=0, keepdims=True) - 1.0
    prompt_row = prompts_ref[sec]
    prompt_pos = jnp.zeros((1, T), F32)
    for d in range(DOCS):
        prompt_pos += jnp.where(doc == d, prompt_row[:, d:d + 1].astype(F32), 0.0)
    position = lane.astype(F32)
    respond = (position - start_pos >= prompt_pos).astype(F32)
    closing = (position == ending).astype(F32)
    later = q_pos - k_pos
    trace = jnp.where((row == col) & (later >= 0),
                      jnp.exp(jnp.maximum(later, 0).astype(F32) * math.log(trace_decay)), 0.0)

    for m in range(1, M):
        pack_copy(m).wait()
    packed = pack_tx[...]
    for m in range(1, M):
        packed = packed + pack_rx[m]
    low_in, low_out = packed[:, :RANK], packed[:, RANK:]
    low_sum = jnp.broadcast_to(jnp.sum(low_in * low_out, axis=1, keepdims=True), (T, T)).T[0:1, :]

    for s, m in pairs:
        score_copy(s, m).wait()

    def section(k):
        slot = lax.rem(sec - k + S, S) * M
        total = score_rx[slot]
        for m in range(1, M):
            total = total + score_rx[slot + m]
        return total[0:1, :]

    base = score_rx[0]
    for m in range(1, M):
        base = base + score_rx[m]
    policy_new = base[1:2, :] + low_sum
    old, ref, reward, value = section(0), section(1), section(2), section(3)
    value8 = jnp.broadcast_to(value, (8, T))
    next_value = jnp.where(lane == T - 1, 0.0, pltpu.roll(value8, T - 1, 1)[0:1, :]) * (1.0 - closing)
    delta = -kl_weight * (old - ref) + closing * reward + next_value - value
    advantage = jnp.sum(trace * jnp.broadcast_to(delta, (T, T)).T, axis=0, keepdims=True)
    count = jnp.sum(respond, axis=1, keepdims=True)
    total = jnp.sum(respond * advantage, axis=1, keepdims=True)
    square = jnp.sum(respond * advantage * advantage, axis=1, keepdims=True)
    mom_rx[0] = jnp.where(sub == 0, count, jnp.where(sub == 1, total, square))

    def mom_copy(s, d):
        k = s * N + d
        return pltpu.make_async_remote_copy(mom_rx.at[0], mom_rx.at[k], m_send.at[k], m_recv.at[k],
                                            device_id=(add(sec, s, S), add(dp, d, N), mp), device_id_type=MESH)

    peers = [(s, d) for s in range(S) for d in range(N) if s or d]
    for s, d in peers:
        mom_copy(s, d).start()
    for s, d in peers:
        mom_copy(s, d).wait()
    moments = jnp.sum(mom_rx[...], axis=0)
    count, total, square = moments[0:1], moments[1:2], moments[2:3]
    mean = total / count
    spread = square / count - mean * mean
    whitened = respond * (advantage - mean) * lax.rsqrt(spread + epsilon)
    adv_ref[...] = whitened
    grad_score = -respond * jnp.exp(policy_new - old) * whitened / count
    gs = jnp.broadcast_to(grad_score, (T, T)).T

    scaled_out = gs[:, :RANK] * low_out
    scaled_in = gs[:, :RANK] * low_in
    turned = jnp.concatenate([scaled_out, scaled_in], axis=1).T
    out_high, out_low = split(turned[:RANK])
    in_t = turned[RANK:].astype(BF16)
    D = rows_ref.shape[1]
    for p in range(S * N):
        lo, hi = p * L, (p + 1) * L
        a, b = min(lo, HQ), min(hi, HQ)
        if b > a:
            high, low = split(patt[:, a:b])
            both[p, :, a - lo:b - lo] = nn(out_high, high) + nn(out_low, high) + nn(out_high, low)
        a, b = max(lo, HQ), min(hi, HQ + D)
        if b > a:
            both[p, :, a - lo:b - lo] = nn(in_t, rows_ref[:, a - HQ:b - HQ])
        a = max(lo, HQ + D)
        if hi > a:
            both[p, :, a - lo:] = jnp.zeros((RANK, hi - a), F32)

    b0, b1 = lax.rem(sec, 2), sec // 2
    near, far = sec + 1 - 2 * b0, lax.rem(sec + half, S)
    Q, H = N, half * N

    def block_copy(src, dst, k, target):
        return pltpu.make_async_remote_copy(src, dst, h_send.at[k], h_recv.at[k],
                                            device_id=(target, dp, mp), device_id_type=MESH)

    tx1[...] = both[pl.ds((1 - b0) * H, H)].astype(BF16)
    copy1 = block_copy(tx1, rx1, 0, near)
    copy1.start()

    so_high, so_low = split(scaled_out)

    def back(c):
        cs = slice(c * HEAD_DIM, (c + 1) * HEAD_DIM)
        down_c = down_ref[:, c * groups * HEAD_DIM:(c + 1) * groups * HEAD_DIM]
        through = nn(so_high, down_c) + nn(so_low, down_c)
        g = jnp.concatenate(
            [gs * chosen_ref[:, (c * groups + i) * HEAD_DIM:(c * groups + i + 1) * HEAD_DIM].astype(F32)
             + through[:, i * HEAD_DIM:(i + 1) * HEAD_DIM] for i in range(groups)], axis=0).astype(BF16)
        p = probs[c]
        k, v = kv_ref[0, :, cs], kv_ref[1, :, cs]
        dprobs = nt(g, v)
        inner = jnp.sum(p * dprobs, axis=-1, keepdims=True)
        ds = (p * (dprobs - inner)).astype(BF16)
        qg = (nn(ds, k) * scale).astype(BF16)
        for i in range(groups):
            qg_ref[:, (c * groups + i) * HEAD_DIM:(c * groups + i + 1) * HEAD_DIM] = qg[i * T:(i + 1) * T]
        mg_ref[0, :, cs] = (tn(ds, stack(q_ref, c)) * scale).astype(BF16)
        mg_ref[1, :, cs] = tn(p.astype(BF16), g).astype(BF16)

    todo = list(range(heads))

    def some(n):
        for _ in range(min(n, len(todo))):
            back(todo.pop(0))

    some(1)
    copy1.wait()
    mine = b0 * H
    tx2[...] = (both[pl.ds(mine + (1 - b1) * Q, Q)] + rx1[pl.ds((1 - b1) * Q, Q)].astype(F32)).astype(BF16)
    def far_copy(d):
        t = add(dp, d, N)
        return pltpu.make_async_remote_copy(tx2.at[t], rx2.at[t], f_send.at[d], f_recv.at[d],
                                            device_id=(far, dp, mp), device_id_type=MESH)

    order = list(range(1, N)) + [0]
    for d in order:
        far_copy(d).start()
    mine = mine + b1 * Q
    both[pl.ds(mine, Q)] += rx1[pl.ds(b1 * Q, Q)].astype(F32)
    some(1)

    def z_copy(d):
        target = add(dp, d, N)
        return pltpu.make_async_remote_copy(txz.at[target], rxz.at[d], z_send.at[d], z_recv.at[d],
                                            device_id=(sec, target, mp), device_id_type=MESH)

    for d in order:
        far_copy(d).wait()
        t = add(dp, d, N)
        part = both[mine + t] + rx2[t].astype(F32)
        if d:
            txz[t] = part.astype(BF16)
            z_copy(d).start()
        else:
            own = part
    some(heads)
    for d in range(1, N):
        z_copy(d).wait()
        own = own + rxz[d].astype(F32)
    fin[mine + dp] = own.astype(BF16)

    def g_copy(d):
        return pltpu.make_async_remote_copy(fin.at[mine + dp], fin.at[mine + dp], g_send.at[d], g_recv.at[d],
                                            device_id=(sec, add(dp, d, N), mp), device_id_type=MESH)

    def a_copy(k, piece, target):
        return pltpu.make_async_remote_copy(fin.at[piece], fin.at[piece], a_send.at[k], a_recv.at[k],
                                            device_id=(target, dp, mp), device_id_type=MESH)

    other = b0 * H + (1 - b1) * Q
    sent = []

    def go(copy):
        copy.start()
        sent.append(copy)

    for d in range(1, N):
        g_copy(d).start()
    for d in range(N):
        source = lax.rem(dp - d + N, N) if d else dp
        if d:
            g_copy(d).wait()
        go(a_copy(d, mine + source, far))
        go(a_copy(N + d, mine + source, near))
    for d in range(N):
        source = lax.rem(dp - d + N, N) if d else dp
        a_copy(d, mine + source, far).wait_recv()
        go(a_copy(2 * N + d, other + source, near))
    for d in range(N):
        a_copy(N + d, mine, near).wait_recv()
        a_copy(2 * N + d, mine, near).wait_recv()
    for copy in sent:
        copy.wait_send()
    sum_ref[...] = fin[...]

    @pl.when(sec >= half)
    def _():
        chosen_copy(chosen_ref, sec, 0, lax.rem(sec, half)).wait_send()

    @pl.when(sec < half)
    def _():
        chosen_copy(chosen_ref, sec, 1, pair).wait_send()
        chosen_copy(chosen_rx.at[sec + half], sec + half, 2, pair).wait_send()


def finish(S, N, L, adv_in, qg_in, mg_in, sum_in, adv_ref, qg_ref, mg_ref, dg_ref, ug_ref):
    adv_ref[...] = adv_in[...]
    qg_ref[...] = qg_in[...]
    mg_ref[...] = mg_in[...]
    HQ, D = dg_ref.shape[1], ug_ref.shape[1]
    for p in range(S * N):
        lo, hi = p * L, (p + 1) * L
        a, b = min(lo, HQ), min(hi, HQ)
        if b > a:
            dg_ref[:, a:b] = sum_in[p, :, a - lo:b - lo].astype(F32)
        a, b = max(lo, HQ), min(hi, HQ + D)
        if b > a:
            ug_ref[:, a - HQ:b - HQ] = sum_in[p, :, a - lo:b - lo].astype(F32)


def outs_shape(T, HQ, KV, RANK, D):
    return (
        jax.ShapeDtypeStruct((1, T), F32),
        jax.ShapeDtypeStruct((T, HQ), BF16),
        jax.ShapeDtypeStruct((2, T, KV), BF16),
        jax.ShapeDtypeStruct((RANK, HQ), F32),
        jax.ShapeDtypeStruct((RANK, D), F32),
    )


def on_device(S, N, M, query, memory, chosen, rows, down, up, squery, skv, score_heads, docs, prompts):
    T, HQ = query.shape[1:]
    KV = memory.shape[3]
    D, RANK = rows.shape[2], down.shape[1]
    heads, groups = KV // HEAD_DIM, HQ // KV
    pieces = S * N
    L = -(-(HQ + D) // (pieces * 128)) * 128
    dma = pltpu.SemaphoreType.DMA
    vm = pltpu.VMEM
    outs = pl.pallas_call(
        functools.partial(kernel, S, N, M, L),
        out_shape=(
            jax.ShapeDtypeStruct((1, T), F32),
            jax.ShapeDtypeStruct((T, HQ), BF16),
            jax.ShapeDtypeStruct((2, T, KV), BF16),
            jax.ShapeDtypeStruct((pieces, RANK, L), BF16),
        ),
        in_specs=[pl.BlockSpec(memory_space=pltpu.VMEM)] * 11,
        out_specs=[pl.BlockSpec(memory_space=pltpu.VMEM)] * 4,
        scratch_shapes=[
            vm((S, heads, groups * T, HEAD_DIM), F32), vm((T, HQ), F32), vm((heads, groups * T, T), F32),
            vm((S, T, HQ), BF16), vm((S, 8, T), F32), vm((S * M, 8, T), F32), vm((T, 2 * RANK), F32),
            vm((M, T, 2 * RANK), F32), vm((pieces, 8, T), F32),
            vm((pieces, RANK, L), F32), vm((pieces // 2, RANK, L), BF16), vm((pieces // 2, RANK, L), BF16),
            vm((N, RANK, L), BF16), vm((N, RANK, L), BF16), vm((N, RANK, L), BF16), vm((N, RANK, L), BF16),
            vm((pieces, RANK, L), BF16), vm((T, T), F32),
            dma((3,)), dma((3,)), dma((S * M,)), dma((S * M,)), dma((M,)), dma((M,)), dma((pieces,)), dma((pieces,)),
            dma((1,)), dma((1,)), dma((N,)), dma((N,)), dma((N,)), dma((N,)), dma((N,)), dma((N,)),
            dma((3 * N,)), dma((3 * N,)),
        ],
        compiler_params=pltpu.CompilerParams(collective_id=0, has_side_effects=True,
                                             vmem_limit_bytes=56 * 1024 * 1024),
    )(query[0], memory[:, 0], chosen[0], rows[0], down.T, up, squery[0, :, 0], skv[0, :, :, 0], score_heads,
      docs, prompts)
    vmem = pl.BlockSpec(memory_space=pltpu.VMEM)
    adv, qg, mg, dg, ug = pl.pallas_call(
        functools.partial(finish, S, N, L),
        out_shape=outs_shape(T, HQ, KV, RANK, D),
        in_specs=[vmem] * 4,
        out_specs=[vmem] * 5,
        compiler_params=pltpu.CompilerParams(vmem_limit_bytes=32 * 1024 * 1024),
    )(*outs)
    return adv, qg[None], mg[:, None], dg.T, ug


def solution(mesh):
    S, N, M = (mesh.shape[a] for a in ("sec", "dp", "mp"))
    return jax.shard_map(
        functools.partial(on_device, S, N, M),
        mesh=mesh,
        in_specs=(
            P(("sec", "dp"), None, "mp"),
            P(None, ("sec", "dp"), None, "mp"),
            P(("sec", "dp"), None, "mp"),
            P(("sec", "dp"), None, "mp"),
            P("mp", None),
            P(None, "mp"),
            P("sec", None, "dp", None, "mp"),
            P("sec", None, None, "dp", None, "mp"),
            P(None, "mp"),
            P(None, "dp", None),
            P(None, "dp", None),
        ),
        out_specs=(
            P(("sec", "dp"), None),
            P(("sec", "dp"), None, "mp"),
            P(None, ("sec", "dp"), None, "mp"),
            P("mp", None),
            P(None, "mp"),
        ),
        check_vma=False,
    )
```
